32 devices in a mesh: row: 8 (over y, x, core), col: 4 (over z).
Axes of the slice: x: 2, y: 2, z: 4, core: 2. Of those that a mesh axis runs over, the one named last changes fastest.
Arguments:
- row_points: bfloat16 [2048, 64], P(('row', 'col')), may hold values from -6 to 6, as said below
- col_points: bfloat16 [16384, 64], P(('col', 'row')), may hold values from -6 to 6, as said below
- row_vectors: bfloat16 [2048, 64], P(('row', 'col')), may hold values from -1 to 1
- col_vectors: bfloat16 [16384, 64], P(('col', 'row')), may hold values from -0.375 to 0.375
- weight_in: bfloat16 [64, 512], replicated, may hold values from -0.75 to 0.75
- bias_in: float32 [512], replicated, may hold values from -3 to 3
- weight_mid: bfloat16 [512, 512], replicated, may hold values from -0.75 to 0.75
- bias_mid: float32 [512], replicated, may hold values from -3 to 3
- weight_out: bfloat16 [512, 256], replicated, may hold values from -0.75 to 0.75
- ard_scales: float32 [256], replicated, may hold values from 0.002 to 0.01
- signal_scale: float32 [1], replicated, may hold values from 0.5 to 2
Outputs:
- row_result: float32 [2048, 64], P(('row', 'col'))
- col_result: float32 [16384, 64], P(('col', 'row'))
The draws below stay inside these ranges and needn't reach their ends.
Inputs may be any that keep to these rules, and one draw needn't show every extreme that they name: `row_points`: each row point's input lies near one of 64 centres that row and column points share; which centre is not given. `col_points`: each column point's input lies near one of the same 64 centres; which centre is not given.
All inputs are finite; a program needn't handle non-finite values.
Results may differ from the reference program's by a relative error of at most 0.0041.
Values may be sent and summed in bfloat16 or wider, within the bound.
No kernel may reach another device: no remote copies, remote signals or barrier semaphores. Data moves between devices by JAX's collectives and lax.ppermute only.
A program may use at most 64 MiB of HBM per device.

```python
import math
import jax
import jax.numpy as jnp
from jax import lax

IN = 64
H = 512
D_EMB = 256
NVEC = 64
NROW = 2048
NCOL = 16384
CENTRES = 64


def shared_centres(key):
    centre_key = jax.random.fold_in(key, 7)
    return jax.random.truncated_normal(centre_key, -3.5, 3.5, (CENTRES, IN), jnp.float32)


def scattered_points(key, point_count, salt_value):
    centres = shared_centres(key)
    labels = jax.random.randint(jax.random.fold_in(key, salt_value), (point_count,), 0, CENTRES)
    near_centre = jnp.take(centres, labels, axis=0)
    jitter_key = jax.random.fold_in(key, salt_value + 1)
    jitter = 0.4 * jax.random.truncated_normal(jitter_key, -3.5, 3.5, (point_count, IN), jnp.float32)
    return (near_centre + jitter).astype(jnp.bfloat16)


def draw_row_points(key, part):
    return scattered_points(key, NROW, 11)


def draw_col_points(key, part):
    return scattered_points(key, NCOL, 23)


def steps_of(own_key, shape, pieces, smallest, top_value):
    level = 1.0
    for position, blocks in pieces:
        steps = jax.random.uniform(jax.random.fold_in(jax.random.fold_in(own_key, 6), position), (blocks,), jnp.float32, smallest / len(pieces), top_value / len(pieces))
        level = level * jnp.repeat(jnp.exp(steps), shape[position] // blocks).reshape((-1,) + (1,) * (len(shape) - 1 - position))
    return level


def scatter_about(own_key, extent, deviation, most, shards=(), kind=jnp.bfloat16):
    loudness = steps_of(own_key, extent, shards, -0.22, 0.18) if shards else 1.0
    entries = jax.random.normal(own_key, extent, jnp.float32) * deviation * loudness
    return jnp.minimum(jnp.maximum(entries, -most), most).astype(kind)


def setup_inputs(seed: int = 0) -> dict:
    arg_keys = jax.random.split(jax.random.key(seed), 12)
    return {
        "row_points": draw_row_points(jax.random.fold_in(arg_keys[11], 71), 0),
        "col_points": draw_col_points(jax.random.fold_in(arg_keys[11], 71), 0),
        "row_vectors": scatter_about(arg_keys[2], (NROW, NVEC), (max(NROW // CENTRES, 1)) ** -0.5, 1.0, ((0, 32),)),
        "col_vectors": scatter_about(arg_keys[3], (NCOL, NVEC), (max(NCOL // CENTRES, 1)) ** -0.5, 0.375, ((0, 32),)),
        "weight_in": scatter_about(arg_keys[4], (IN, H), IN ** -0.5, 0.75),
        "bias_in": scatter_about(arg_keys[5], (H,), 0.5, 3.0, (), jnp.float32),
        "weight_mid": scatter_about(arg_keys[6], (H, H), (H // 8) ** -0.5, 0.75),
        "bias_mid": scatter_about(arg_keys[7], (H,), 0.5, 3.0, (), jnp.float32),
        "weight_out": scatter_about(arg_keys[8], (H, D_EMB), (H // 8) ** -0.5, 0.75),
        "ard_scales": jnp.clip(jnp.exp(jax.random.uniform(arg_keys[9], (D_EMB,), jnp.float32, math.log(0.002), math.log(0.01))), 0.002, 0.01),
        "signal_scale": jnp.clip(jnp.exp(jax.random.uniform(arg_keys[10], (1,), jnp.float32, math.log(0.5), math.log(2.0))), 0.5, 2.0),
    }


def embed_points(points, weight_in, bias_in, weight_mid, bias_mid, weight_out, ard_scales):
    hidden_one = jnp.tanh(jnp.dot(points, weight_in, preferred_element_type=jnp.float32) + bias_in).astype(jnp.bfloat16)
    hidden_two = jnp.tanh(jnp.dot(hidden_one, weight_mid, preferred_element_type=jnp.float32) + bias_mid).astype(jnp.bfloat16)
    return (jnp.dot(hidden_two, weight_out, preferred_element_type=jnp.float32) * jnp.sqrt(ard_scales)).astype(jnp.bfloat16)

def reference(row_points, col_points, row_vectors, col_vectors, weight_in, bias_in, weight_mid, bias_mid, weight_out, ard_scales, signal_scale):
    row_feats = embed_points(row_points, weight_in, bias_in, weight_mid, bias_mid, weight_out, ard_scales)
    col_feats = embed_points(col_points, weight_in, bias_in, weight_mid, bias_mid, weight_out, ard_scales)
    row_sq = lax.optimization_barrier(jnp.sum(jnp.square(row_feats.astype(jnp.float32)), axis=1))
    col_sq = lax.optimization_barrier(jnp.sum(jnp.square(col_feats.astype(jnp.float32)), axis=1))
    width_cols = math.gcd(NCOL, 1024)
    groups = NCOL // width_cols
    feat_groups = col_feats.reshape(groups, width_cols, D_EMB)
    vector_groups = col_vectors.reshape(groups, width_cols, NVEC)
    square_groups = col_sq.reshape(groups, width_cols)

    def visit(totals, inputs):
        feats_now, vectors_now, squares_now = inputs
        inner_prod = lax.dot_general(row_feats, feats_now, (((1,), (1,)), ((), ())), preferred_element_type=jnp.float32)
        kernel = jnp.exp(inner_prod - 0.5 * row_sq[:, None] - 0.5 * squares_now[None, :]).astype(jnp.bfloat16)
        totals = totals + jnp.dot(kernel, vectors_now, preferred_element_type=jnp.float32)
        col_part = lax.dot_general(kernel, row_vectors, (((0,), (0,)), ((), ())), preferred_element_type=jnp.float32)
        return (totals, col_part)
    row_total, col_parts = lax.scan(visit, jnp.zeros((NROW, NVEC), jnp.float32), (feat_groups, vector_groups, square_groups))
    return (signal_scale[0] * row_total, signal_scale[0] * col_parts.reshape(NCOL, NVEC))
```

```python
import functools

import jax
import jax.numpy as jnp
from jax import lax
from jax.experimental import pallas as pl
from jax.experimental.pallas import tpu as pltpu
from jax.sharding import PartitionSpec as P

AXES = ("row", "col")
F32, BF16 = jnp.float32, jnp.bfloat16


def dot(a, b, over):
    return lax.dot_general(a, b, (over, ((), ())), preferred_element_type=F32)


def embed(points, over, w_in, b_in, w_mid, b_mid, w_out, ard):
    one = jnp.tanh(dot(points, w_in[...], ((over,), (0,))) + b_in[...]).astype(BF16)
    two = jnp.tanh(dot(one, w_mid[...], ((1,), (0,))) + b_mid[...]).astype(BF16)
    return (dot(two, w_out[...], ((1,), (0,))) * jnp.sqrt(ard[...])).astype(BF16)


def col_kernel(chunk, points, w_in, b_in, w_mid, b_mid, w_out, ard, feats, half_sq):
    for start in range(0, points.shape[1], chunk):
        part = pl.ds(start, chunk)
        turned = embed(points[:, part], 0, w_in, b_in, w_mid, b_mid, w_out, ard).T
        feats[:, part] = turned
        half_sq[:, part] = 0.5 * jnp.sum(jnp.square(turned.astype(F32)), axis=0, keepdims=True)


def panel_kernel(chunk_rows, chunk_cols, rows, feats, half_sq, col_vecs, w_in, b_in, w_mid, b_mid, w_out, ard, *rest):
    row_out, near, far = rest[-3:]
    before = rest[:-3]
    width = w_in.shape[0]
    count_rows, count_cols = rows.shape[0], feats.shape[1]
    for at in range(0, count_rows, chunk_rows):
        block = rows[at : at + chunk_rows, :]
        row_feats = embed(block[:, :width], 1, w_in, b_in, w_mid, b_mid, w_out, ard)
        row_half = 0.5 * jnp.sum(jnp.square(row_feats.astype(F32)), axis=1, keepdims=True)
        vecs = block[:, width:]
        row_acc = None
        for start in range(0, count_cols, chunk_cols):
            part = pl.ds(start, chunk_cols)
            inner = dot(row_feats, feats[:, part], ((1,), (0,)))
            kernel = jnp.exp(inner - row_half - half_sq[:, part]).astype(BF16)
            term = dot(kernel, col_vecs[:, part], ((1,), (1,)))
            row_acc = term if row_acc is None else row_acc + term
            col_term = dot(vecs, kernel, ((0,), (0,)))
            side = 0 if start < count_cols // 2 else 1
            out = (near, far)[side]
            here = pl.ds(start - side * (count_cols // 2), chunk_cols)
            if at > 0:
                col_term = col_term + out[:, here]
            elif before:
                col_term = col_term + before[side][:, here]
            out[:, here] = col_term
        row_out[at : at + chunk_rows, :] = row_acc


def call(kernel, outs, args, flops):
    return pl.pallas_call(
        kernel,
        out_shape=outs,
        in_specs=[pl.BlockSpec(memory_space=pltpu.VMEM)] * len(args),
        out_specs=[pl.BlockSpec(memory_space=pltpu.VMEM)] * len(outs),
        compiler_params=pltpu.CompilerParams(vmem_limit_bytes=40 * 2**20),
        cost_estimate=pl.CostEstimate(flops=flops, bytes_accessed=2**20, transcendentals=0),
    )(*args)


def body(
    row_points,
    col_points,
    row_vectors,
    col_vectors,
    weight_in,
    bias_in,
    weight_mid,
    bias_mid,
    weight_out,
    ard_scales,
    signal_scale,
):
    count_row, count_col = lax.axis_size("row"), lax.axis_size("col")
    devices = count_row * count_col
    row_masks = [1 << b for b in reversed(range(count_col.bit_length() - 1))] + [devices // 2]
    col_masks = [count_col << b for b in reversed(range(count_row.bit_length() - 2))]

    def swap(block, mask):
        return lax.ppermute(block, AXES, [(i, i ^ mask) for i in range(devices)])

    weights = (
        weight_in,
        bias_in.reshape(1, -1),
        weight_mid,
        bias_mid.reshape(1, -1),
        weight_out,
        ard_scales.reshape(1, -1),
    )
    rows = jnp.concatenate([row_points, row_vectors], axis=1)
    points, vectors = col_points.T, col_vectors.T
    for mask in col_masks:
        points = jnp.concatenate([points, swap(points, mask)], axis=1)
        vectors = jnp.concatenate([vectors, swap(vectors, mask)], axis=1)
    for mask in row_masks[:-1]:
        rows = jnp.concatenate([rows, swap(rows, mask)], axis=0)
    far_rows = swap(rows, row_masks[-1])

    count_rows, count_cols = rows.shape[0], points.shape[1]
    nvec, emb = vectors.shape[0], weight_out.shape[1]
    chunk_cols, chunk_rows = min(512, count_cols // 2), min(256, count_rows)
    layers = sum(w.shape[0] * w.shape[1] for w in (weight_in, weight_mid, weight_out))
    feats, half_sq = call(
        functools.partial(col_kernel, chunk_cols),
        [jax.ShapeDtypeStruct((emb, count_cols), BF16), jax.ShapeDtypeStruct((1, count_cols), F32)],
        (points, *weights),
        2 * count_cols * layers,
    )
    half = jax.ShapeDtypeStruct((nvec, count_cols // 2), F32)
    panel = functools.partial(
        call,
        functools.partial(panel_kernel, chunk_rows, chunk_cols),
        [jax.ShapeDtypeStruct((count_rows, nvec), F32), half, half],
        flops=2 * count_rows * (layers + count_cols * (emb + 8 * nvec)),
    )
    row_near, near, far = panel((rows, feats, half_sq, vectors, *weights))
    row_far, near, far = panel((far_rows, feats, half_sq, vectors, *weights, near, far))

    row_sum = row_near + swap(row_far, row_masks[-1])
    for mask in reversed(row_masks[:-1]):
        keep, give = jnp.split(row_sum, 2, axis=0)
        row_sum = keep + swap(give, mask)
    col_sum = near + swap(far, col_masks[-1])
    for mask in reversed(col_masks[:-1]):
        keep, give = jnp.split(col_sum, 2, axis=1)
        col_sum = keep + swap(give, mask)
    return (row_sum * signal_scale[0], col_sum.T * signal_scale[0])


def solution(mesh):
    in_specs = (
        P(("row", "col"), None),
        P(("col", "row"), None),
        P(("row", "col"), None),
        P(("col", "row"), None),
        P(),
        P(),
        P(),
        P(),
        P(),
        P(),
        P(),
    )
    out_specs = (P(("row", "col"), None), P(("col", "row"), None))
    return jax.shard_map(body, mesh=mesh, in_specs=in_specs, out_specs=out_specs, check_vma=False)
```

```python
import functools

import jax
import jax.numpy as jnp
from jax import lax
from jax.experimental import pallas as pl
from jax.experimental.pallas import tpu as pltpu
from jax.sharding import PartitionSpec as P

AXES = ("row", "col")
F32, BF16 = jnp.float32, jnp.bfloat16


def dot(a, b, over):
    return lax.dot_general(a, b, (over, ((), ())), preferred_element_type=F32)


def embed(points, over, w_in, b_in, w_mid, b_mid, w_out, ard):
    one = jnp.tanh(dot(points, w_in[...], ((over,), (0,))) + b_in[...]).astype(BF16)
    two = jnp.tanh(dot(one, w_mid[...], ((1,), (0,))) + b_mid[...]).astype(BF16)
    return (dot(two, w_out[...], ((1,), (0,))) * jnp.sqrt(ard[...])).astype(BF16)


def col_kernel(chunk, points, w_in, b_in, w_mid, b_mid, w_out, ard, feats, half_sq):
    for start in range(0, points.shape[1], chunk):
        part = pl.ds(start, chunk)
        turned = embed(points[:, part], 0, w_in, b_in, w_mid, b_mid, w_out, ard).T
        feats[:, part] = turned
        half_sq[:, part] = 0.5 * jnp.sum(jnp.square(turned.astype(F32)), axis=0, keepdims=True)


def panel_kernel(chunk_rows, chunk_cols, tall, sides, rows, *rest):
    columns = [rest[3 * side : 3 * side + 3] for side in range(sides)]
    weights, rest = rest[3 * sides : 3 * sides + 6], rest[3 * sides + 6 :]
    before, row_out, col_outs = rest[: -sides - 1], rest[-sides - 1], rest[-sides:]
    width = weights[0].shape[0]
    own = rows.shape[1] - width
    for at in range(0, rows.shape[0], chunk_rows):
        block = rows[at : at + chunk_rows, :]
        row_feats = embed(block[:, :width], 1, *weights)
        row_half = 0.5 * jnp.sum(jnp.square(row_feats.astype(F32)), axis=1, keepdims=True)
        vecs = block[:, width:]
        row_acc = None
        for side, (feats, half_sq, col_vecs) in enumerate(columns):
            for start in range(0, feats.shape[1], chunk_cols):
                part = pl.ds(start, chunk_cols)
                inner = dot(row_feats, feats[:, part], ((1,), (0,)))
                kernel = jnp.exp(inner - row_half - half_sq[:, part]).astype(BF16)
                term = dot(kernel, col_vecs[:, part], ((1,), (1,)))
                row_acc = term if row_acc is None else row_acc + term
                col_term = dot(vecs, kernel, ((0,), (0,)))
                if at > 0:
                    col_term = col_term + col_outs[side][:, part]
                elif before:
                    col_term = col_term + before[side][:, part]
                col_outs[side][:, part] = col_term
        for pair in range(0, chunk_rows, 2 * tall):
            to = pl.ds((at + pair) // 2, tall)
            row_out[to, :own] = row_acc[pair : pair + tall]
            row_out[to, own:] = row_acc[pair + tall : pair + 2 * tall]


def call(kernel, outs, args, flops):
    return pl.pallas_call(
        kernel,
        out_shape=outs,
        in_specs=[pl.BlockSpec(memory_space=pltpu.VMEM)] * len(args),
        out_specs=[pl.BlockSpec(memory_space=pltpu.VMEM)] * len(outs),
        compiler_params=pltpu.CompilerParams(vmem_limit_bytes=40 * 2**20),
        cost_estimate=pl.CostEstimate(flops=flops, bytes_accessed=2**20, transcendentals=0),
    )(*args)


def body(
    row_points,
    col_points,
    row_vectors,
    col_vectors,
    weight_in,
    bias_in,
    weight_mid,
    bias_mid,
    weight_out,
    ard_scales,
    signal_scale,
):
    count_row, count_col = lax.axis_size("row"), lax.axis_size("col")
    devices = count_row * count_col
    row_masks = [1 << b for b in reversed(range(count_col.bit_length() - 1))] + [devices // 2]
    col_masks = [count_col << b for b in reversed(range(count_row.bit_length() - 2))]

    def swap(block, mask):
        return lax.ppermute(block, AXES, [(i, i ^ mask) for i in range(devices)])

    weights = (
        weight_in,
        bias_in.reshape(1, -1),
        weight_mid,
        bias_mid.reshape(1, -1),
        weight_out,
        ard_scales.reshape(1, -1),
    )
    block, nvec = row_vectors.shape
    emb = weight_out.shape[1]
    layers = sum(w.shape[0] * w.shape[1] for w in (weight_in, weight_mid, weight_out))
    chunk_cols = min(512, col_points.shape[0])

    def col_feats(points):
        count = points.shape[1]
        return call(
            functools.partial(col_kernel, chunk_cols),
            [jax.ShapeDtypeStruct((emb, count), BF16), jax.ShapeDtypeStruct((1, count), F32)],
            (points, *weights),
            2 * count * layers,
        )

    rows = jnp.concatenate([row_points, row_vectors], axis=1)
    rows = jnp.concatenate([rows, swap(rows, row_masks[0])], axis=0)
    points, vectors = [col_points.T], [col_vectors.T]
    feats = [col_feats(points[0])]
    for mask in col_masks:
        points.append(swap(jnp.concatenate(points, axis=1), mask))
        vectors.append(swap(jnp.concatenate(vectors, axis=1), mask))
        if mask == col_masks[0]:
            rows, points[1], feats[0] = lax.optimization_barrier((rows, points[1], feats[0]))
        feats.append(col_feats(points[-1]))
    for mask in row_masks[1:-1]:
        rows = jnp.concatenate([rows, swap(rows, mask)], axis=0)
    rows, feats = lax.optimization_barrier((rows, feats))
    far_rows = swap(rows, row_masks[-1])

    count_rows = rows.shape[0]
    sides = [v.shape[1] for v in vectors]
    panel = functools.partial(
        call,
        functools.partial(panel_kernel, min(4 * block, count_rows), chunk_cols, block, len(sides)),
        [jax.ShapeDtypeStruct((count_rows // 2, 2 * nvec), F32)]
        + [jax.ShapeDtypeStruct((nvec, count), F32) for count in sides],
        flops=2 * count_rows * (layers + sum(sides) * (emb + 8 * nvec)),
    )
    columns = [a for f, v in zip(feats, vectors, strict=True) for a in (*f, v)]
    row_near, *near = panel((rows, *columns, *weights))
    row_far, *col_sums = panel((far_rows, *columns, *weights, *near))

    row_sum = row_near + swap(row_far, row_masks[-1])
    for number, mask in reversed(list(enumerate(col_masks))):
        got, start = swap(col_sums[number + 1], mask), 0
        for side in range(number + 1):
            col_sums[side] = col_sums[side] + got[:, start : start + sides[side]]
            start += sides[side]
    for mask in reversed(row_masks[1:-1]):
        keep, give = jnp.split(row_sum, 2, axis=0)
        row_sum = keep + swap(give, mask)
    row_sum, col_sum = lax.optimization_barrier((row_sum, col_sums[0]))
    row_sum = row_sum[:, :nvec] + swap(row_sum, row_masks[0])[:, nvec:]
    return (row_sum * signal_scale[0], col_sum.T * signal_scale[0])


def solution(mesh):
    in_specs = (
        P(("row", "col"), None),
        P(("col", "row"), None),
        P(("row", "col"), None),
        P(("col", "row"), None),
        P(),
        P(),
        P(),
        P(),
        P(),
        P(),
        P(),
    )
    out_specs = (P(("row", "col"), None), P(("col", "row"), None))
    return jax.shard_map(body, mesh=mesh, in_specs=in_specs, out_specs=out_specs, check_vma=False)
```

```python
import functools

import jax
import jax.numpy as jnp
from jax import lax
from jax.experimental import pallas as pl
from jax.experimental.pallas import tpu as pltpu
from jax.sharding import PartitionSpec as P

AXES = ("row", "col")
F32, BF16 = jnp.float32, jnp.bfloat16
HOLD_FLOPS = 2 * 10**10
FINISH_FLOPS = 10**6


def dot(a, b, over):
    return lax.dot_general(a, b, (over, ((), ())), preferred_element_type=F32)


def embed(points, over, w_in, b_in, w_mid, b_mid, w_out, ard):
    one = jnp.tanh(dot(points, w_in[...], ((over,), (0,))) + b_in[...]).astype(BF16)
    two = jnp.tanh(dot(one, w_mid[...], ((1,), (0,))) + b_mid[...]).astype(BF16)
    return (dot(two, w_out[...], ((1,), (0,))) * jnp.sqrt(ard[...])).astype(BF16)


def col_kernel(chunk, points, w_in, b_in, w_mid, b_mid, w_out, ard, feats, half_sq):
    for start in range(0, points.shape[1], chunk):
        part = pl.ds(start, chunk)
        turned = embed(points[:, part], 0, w_in, b_in, w_mid, b_mid, w_out, ard).T
        feats[:, part] = turned
        half_sq[:, part] = 0.5 * jnp.sum(jnp.square(turned.astype(F32)), axis=0, keepdims=True)


def panel_kernel(chunk_rows, chunk_cols, tall, sides, rows, *rest):
    columns = [rest[3 * side : 3 * side + 3] for side in range(sides)]
    weights, rest = rest[3 * sides : 3 * sides + 6], rest[3 * sides + 6 :]
    before, row_out, col_outs = rest[: -sides - 1], rest[-sides - 1], rest[-sides:]
    width = weights[0].shape[0]
    own = rows.shape[1] - width
    for at in range(0, rows.shape[0], chunk_rows):
        block = rows[at : at + chunk_rows, :]
        row_feats = embed(block[:, :width], 1, *weights)
        row_half = 0.5 * jnp.sum(jnp.square(row_feats.astype(F32)), axis=1, keepdims=True)
        vecs = block[:, width:]
        row_acc = None
        for side, (feats, half_sq, col_vecs) in enumerate(columns):
            for start in range(0, feats.shape[1], chunk_cols):
                part = pl.ds(start, chunk_cols)
                inner = dot(row_feats, feats[:, part], ((1,), (0,)))
                kernel = jnp.exp(inner - row_half - half_sq[:, part]).astype(BF16)
                term = dot(kernel, col_vecs[:, part], ((1,), (1,)))
                row_acc = term if row_acc is None else row_acc + term
                col_term = dot(vecs, kernel, ((0,), (0,)))
                if at > 0:
                    col_term = col_term + col_outs[side][:, part]
                elif before:
                    col_term = col_term + before[side][:, part]
                col_outs[side][:, part] = col_term
        for pair in range(0, chunk_rows, 2 * tall):
            to = pl.ds((at + pair) // 2, tall)
            row_out[to, :own] = row_acc[pair : pair + tall]
            row_out[to, own:] = row_acc[pair + tall : pair + 2 * tall]


def call(kernel, outs, args, flops):
    return pl.pallas_call(
        kernel,
        out_shape=outs,
        in_specs=[pl.BlockSpec(memory_space=pltpu.VMEM)] * len(args),
        out_specs=[pl.BlockSpec(memory_space=pltpu.VMEM)] * len(outs),
        compiler_params=pltpu.CompilerParams(vmem_limit_bytes=16 * 2**20),
        cost_estimate=pl.CostEstimate(flops=flops, bytes_accessed=2**20, transcendentals=0),
    )(*args)


def hold_kernel(rows, out):
    out[...] = rows[...]


def finish_kernel(scale, own, got, result):
    result[...] = (own[...] + got[...]) * scale[...]


def body(
    row_points,
    col_points,
    row_vectors,
    col_vectors,
    weight_in,
    bias_in,
    weight_mid,
    bias_mid,
    weight_out,
    ard_scales,
    signal_scale,
):
    count_row, count_col = lax.axis_size("row"), lax.axis_size("col")
    devices = count_row * count_col
    row_masks = [1 << b for b in reversed(range(count_col.bit_length() - 1))] + [devices // 2]
    col_masks = [count_col << b for b in reversed(range(count_row.bit_length() - 2))]

    def swap(block, mask):
        return lax.ppermute(block, AXES, [(i, i ^ mask) for i in range(devices)])

    weights = (
        weight_in,
        bias_in.reshape(1, -1),
        weight_mid,
        bias_mid.reshape(1, -1),
        weight_out,
        ard_scales.reshape(1, -1),
        signal_scale.reshape(1, 1),
    )
    block, nvec = row_vectors.shape
    emb = weight_out.shape[1]
    layers = sum(w.shape[0] * w.shape[1] for w in (weight_in, weight_mid, weight_out))
    chunk_cols = min(512, col_points.shape[0])

    def col_feats(points):
        count = points.shape[1]
        return call(
            functools.partial(col_kernel, chunk_cols),
            [jax.ShapeDtypeStruct((emb, count), BF16), jax.ShapeDtypeStruct((1, count), F32)],
            (points, *weights),
            2 * count * layers,
        )

    rows = jnp.concatenate([row_points, row_vectors], axis=1)
    (rows,) = call(hold_kernel, [jax.ShapeDtypeStruct(rows.shape, BF16)], (rows,), HOLD_FLOPS)
    *weights, scale = weights
    for mask in row_masks[:-2]:
        rows = jnp.concatenate([rows, swap(rows, mask)], axis=0)
    points, vectors = [col_points.T], [col_vectors.T]
    for mask in col_masks:
        points.append(swap(jnp.concatenate(points, axis=1), mask))
        vectors.append(swap(jnp.concatenate(vectors, axis=1), mask))
    feats = [col_feats(p) for p in points[:-1]]
    rows = jnp.concatenate([rows, swap(rows, row_masks[-2])], axis=0)
    rows, feats = lax.optimization_barrier((rows, feats))
    far_rows = swap(rows, row_masks[-1])
    feats.append(col_feats(points[-1]))
    far_rows, feats = lax.optimization_barrier((far_rows, feats))

    count_rows = rows.shape[0]
    sides = [v.shape[1] for v in vectors]
    panel = functools.partial(
        call,
        functools.partial(panel_kernel, min(4 * block, count_rows), chunk_cols, block, len(sides)),
        [jax.ShapeDtypeStruct((count_rows // 2, 2 * nvec), F32)]
        + [jax.ShapeDtypeStruct((nvec, count), F32) for count in sides],
        flops=2 * count_rows * (layers + sum(sides) * (emb + 8 * nvec)),
    )
    columns = [a for f, v in zip(feats, vectors, strict=True) for a in (*f, v)]
    row_far, *far = panel((far_rows, *columns, *weights))
    row_near, *col_sums = panel((rows, *columns, *weights, *far))

    got, col_sums = lax.optimization_barrier((swap(row_far, row_masks[-1]), col_sums))
    row_sum = row_near + got
    for number, mask in reversed(list(enumerate(col_masks))[1:]):
        got, start = swap(col_sums[number + 1], mask), 0
        for side in range(number + 1):
            col_sums[side] = col_sums[side] + got[:, start : start + sides[side]]
            start += sides[side]
    got = swap(col_sums[1], col_masks[0])
    (col_result,) = call(
        finish_kernel, [jax.ShapeDtypeStruct(got.shape, F32)], (scale, col_sums[0], got), FINISH_FLOPS
    )
    for mask in reversed(row_masks[1:-1]):
        keep, give = jnp.split(row_sum, 2, axis=0)
        row_sum = keep + swap(give, mask)
    got, col_result = lax.optimization_barrier((swap(row_sum, row_masks[0]), col_result))
    row_sum = row_sum[:, :nvec] + got[:, nvec:]
    return (row_sum * scale, col_result.T)


def solution(mesh):
    in_specs = (
        P(("row", "col"), None),
        P(("col", "row"), None),
        P(("row", "col"), None),
        P(("col", "row"), None),
        P(),
        P(),
        P(),
        P(),
        P(),
        P(),
        P(),
    )
    out_specs = (P(("row", "col"), None), P(("col", "row"), None))
    return jax.shard_map(body, mesh=mesh, in_specs=in_specs, out_specs=out_specs, check_vma=False)
```

```python
import functools

import jax
import jax.numpy as jnp
from jax import lax
from jax.experimental import pallas as pl
from jax.experimental.pallas import tpu as pltpu
from jax.sharding import PartitionSpec as P

AXES = ("row", "col")
F32, BF16 = jnp.float32, jnp.bfloat16
HOLD_FLOPS = 2 * 10**10
FINISH_FLOPS = 10**6


def dot(a, b, over):
    return lax.dot_general(a, b, (over, ((), ())), preferred_element_type=F32)


def embed(points, over, w_in, b_in, w_mid, b_mid, w_out, ard):
    one = jnp.tanh(dot(points, w_in[...], ((over,), (0,))) + b_in[...]).astype(BF16)
    two = jnp.tanh(dot(one, w_mid[...], ((1,), (0,))) + b_mid[...]).astype(BF16)
    return (dot(two, w_out[...], ((1,), (0,))) * jnp.sqrt(ard[...])).astype(BF16)


def col_kernel(chunk, points, *rest):
    weights, (feats, half_sq) = rest[:6], rest[-2:]
    for start in range(0, points.shape[1], chunk):
        part = pl.ds(start, chunk)
        turned = embed(points[:, part], 0, *weights).T
        feats[:, part] = turned
        half_sq[:, part] = 0.5 * jnp.sum(jnp.square(turned.astype(F32)), axis=0, keepdims=True)


def panel_kernel(chunk_rows, chunk_cols, tall, sides, rows, *rest):
    columns = [rest[3 * side : 3 * side + 3] for side in range(sides)]
    weights, rest = rest[3 * sides : 3 * sides + 6], rest[3 * sides + 6 :]
    keep = len(rest) == 1 + sides
    if keep:
        row_out, *panels = rest
    else:
        others, panels, row_out, col_outs = rest[0], rest[1 : 1 + sides], rest[1 + sides], rest[2 + sides :]
    width = weights[0].shape[0]
    own = rows.shape[1] - width
    for at in range(0, rows.shape[0], chunk_rows):
        here = pl.ds(at, chunk_rows)
        block = rows[here, :]
        row_feats = embed(block[:, :width], 1, *weights)
        row_half = 0.5 * jnp.sum(jnp.square(row_feats.astype(F32)), axis=1, keepdims=True)
        row_acc = None
        for side, (feats, half_sq, col_vecs) in enumerate(columns):
            for start in range(0, feats.shape[1], chunk_cols):
                part = pl.ds(start, chunk_cols)
                inner = dot(row_feats, feats[:, part], ((1,), (0,)))
                kernel = jnp.exp(inner - row_half - half_sq[:, part]).astype(BF16)
                term = dot(kernel, col_vecs[:, part], ((1,), (1,)))
                row_acc = term if row_acc is None else row_acc + term
                if keep:
                    panels[side][here, part] = kernel
                else:
                    col_term = dot(block[:, width:], kernel, ((0,), (0,)))
                    col_term += dot(others[here, width:], panels[side][here, part], ((0,), (0,)))
                    if at > 0:
                        col_term += col_outs[side][:, part]
                    col_outs[side][:, part] = col_term
        for start in range(0, chunk_rows, 2 * tall):
            to = pl.ds((at + start) // 2, tall)
            row_out[to, :own] = row_acc[start : start + tall]
            row_out[to, own:] = row_acc[start + tall : start + 2 * tall]


def call(kernel, outs, args, flops):
    return pl.pallas_call(
        kernel,
        out_shape=outs,
        in_specs=[pl.BlockSpec(memory_space=pltpu.VMEM)] * len(args),
        out_specs=[pl.BlockSpec(memory_space=pltpu.VMEM)] * len(outs),
        compiler_params=pltpu.CompilerParams(vmem_limit_bytes=20 * 2**20),
        cost_estimate=pl.CostEstimate(flops=flops, bytes_accessed=2**20, transcendentals=0),
    )(*args)


def hold_kernel(rows, out):
    out[...] = rows[...]


def finish_kernel(scale, own, got, result):
    result[...] = (own[...] + got[...]) * scale[...]


def finish_rows_kernel(scale, own, got, result):
    tall, width = got.shape[0], result.shape[1]
    total = (own[:tall, :] + got[...]) * scale[...]
    result[:tall, :] = total[:, :width]
    result[tall:, :] = total[:, width:]


def body(
    row_points,
    col_points,
    row_vectors,
    col_vectors,
    weight_in,
    bias_in,
    weight_mid,
    bias_mid,
    weight_out,
    ard_scales,
    signal_scale,
):
    count_row, count_col = lax.axis_size("row"), lax.axis_size("col")
    devices = count_row * count_col
    row_masks = [1 << b for b in reversed(range(count_col.bit_length() - 1))] + [devices // 2]
    col_masks = [count_col << b for b in reversed(range(count_row.bit_length() - 2))]

    def swap(block, mask):
        return lax.ppermute(block, AXES, [(i, i ^ mask) for i in range(devices)])

    weights = (
        weight_in,
        bias_in.reshape(1, -1),
        weight_mid,
        bias_mid.reshape(1, -1),
        weight_out,
        ard_scales.reshape(1, -1),
        signal_scale.reshape(1, 1),
    )
    block, nvec = row_vectors.shape
    emb = weight_out.shape[1]
    layers = sum(w.shape[0] * w.shape[1] for w in (weight_in, weight_mid, weight_out))
    chunk_cols = min(512, col_points.shape[0])

    def col_feats(points):
        count = points.shape[1]
        return call(
            functools.partial(col_kernel, chunk_cols),
            [jax.ShapeDtypeStruct((emb, count), BF16), jax.ShapeDtypeStruct((1, count), F32)],
            (points, *weights),
            2 * count * layers,
        )

    *weights, scale = weights
    rows = jnp.concatenate([row_points, row_vectors], axis=1)
    (got,) = call(hold_kernel, [jax.ShapeDtypeStruct(rows.shape, BF16)], (swap(rows, row_masks[0]),), HOLD_FLOPS)
    rows = jnp.concatenate([rows, got], axis=0)
    for mask in row_masks[1:-2]:
        rows = jnp.concatenate([rows, swap(rows, mask)], axis=0)
    points, vectors = [col_points.T], [col_vectors.T]
    for mask in col_masks:
        points.append(swap(jnp.concatenate(points, axis=1), mask))
    feats = [col_feats(points[0])]
    got, feats = lax.optimization_barrier((swap(rows, row_masks[-2]), feats))
    rows = jnp.concatenate([rows, got], axis=0)
    far_rows = swap(rows, row_masks[-1])
    feats += [col_feats(p) for p in points[1:]]
    for mask in col_masks:
        vectors.append(jnp.concatenate([swap(v, mask) for v in vectors], axis=1))
    far_rows, feats = lax.optimization_barrier((far_rows, feats))

    count_rows = rows.shape[0]
    sides = [v.shape[1] for v in vectors]
    panel = functools.partial(panel_kernel, min(4 * block, count_rows), chunk_cols, block // 2, len(sides))
    columns = [a for f, v in zip(feats, vectors, strict=True) for a in (*f, v)]
    flops = 2 * count_rows * (layers + sum(sides) * (emb + 4 * nvec))
    sums = jax.ShapeDtypeStruct((count_rows // 2, 2 * nvec), F32)
    far_panels = [jax.ShapeDtypeStruct((count_rows, count), BF16) for count in sides]
    row_far, *far_panels = call(panel, [sums, *far_panels], (far_rows, *columns, *weights), flops)
    col_sums = [jax.ShapeDtypeStruct((nvec, count), F32) for count in sides]
    args = (rows, *columns, *weights, far_rows, *far_panels)
    row_near, *col_sums = call(panel, [sums, *col_sums], args, flops)

    got, col_sums = lax.optimization_barrier((swap(row_far, row_masks[-1]), col_sums))
    row_sum = row_near + got
    for number, mask in reversed(list(enumerate(col_masks))[1:]):
        got, start = swap(col_sums[number + 1], mask), 0
        for side in range(number + 1):
            col_sums[side] = col_sums[side] + got[:, start : start + sides[side]]
            start += sides[side]
    got = swap(col_sums[1], col_masks[0])
    (col_result,) = call(
        finish_kernel, [jax.ShapeDtypeStruct(got.shape, F32)], (scale, col_sums[0], got), FINISH_FLOPS
    )
    for mask in reversed(row_masks[1:-1]):
        keep, give = jnp.split(row_sum, 2, axis=0)
        row_sum = keep + swap(give, mask)
    got, col_result = lax.optimization_barrier((swap(row_sum[block // 2 :], row_masks[0]), col_result))
    (row_result,) = call(
        finish_rows_kernel, [jax.ShapeDtypeStruct((block, nvec), F32)], (scale, row_sum, got), FINISH_FLOPS
    )
    return (row_result, col_result.T)


def solution(mesh):
    in_specs = (
        P(("row", "col"), None),
        P(("col", "row"), None),
        P(("row", "col"), None),
        P(("col", "row"), None),
        P(),
        P(),
        P(),
        P(),
        P(),
        P(),
        P(),
    )
    out_specs = (P(("row", "col"), None), P(("col", "row"), None))
    return jax.shard_map(body, mesh=mesh, in_specs=in_specs, out_specs=out_specs, check_vma=False)
```

```python
import functools
import math

import jax
import jax.numpy as jnp
from jax import lax
from jax.experimental import pallas as pl
from jax.experimental.pallas import tpu as pltpu
from jax.sharding import PartitionSpec as P

AXES = ("row", "col")
F32, BF16 = jnp.float32, jnp.bfloat16
HOLD_FLOPS = 2 * 10**10
CUT_MOST = 0.375 * 1.0625
FINISH_FLOPS = 10**6


def dot(a, b, over):
    return lax.dot_general(a, b, (over, ((), ())), preferred_element_type=F32)


def embed(points, over, w_in, b_in, w_mid, b_mid, w_out, ard):
    one = jnp.tanh(dot(points, w_in[...], ((over,), (0,))) + b_in[...]).astype(BF16)
    two = jnp.tanh(dot(one, w_mid[...], ((1,), (0,))) + b_mid[...]).astype(BF16)
    return (dot(two, w_out[...], ((1,), (0,))) * jnp.sqrt(ard[...])).astype(BF16)


def col_kernel(chunk, points, *rest):
    weights, (feats, half_sq) = rest[:6], rest[-2:]
    for start in range(0, points.shape[1], chunk):
        part = pl.ds(start, chunk)
        turned = embed(points[:, part], 0, *weights).T
        feats[:, part] = turned
        half_sq[:, part] = 0.5 * jnp.sum(jnp.square(turned.astype(F32)), axis=0, keepdims=True)


def panel_kernel(chunk_rows, chunk_cols, tall, sides, rows, *rest):
    columns = [rest[3 * side : 3 * side + 3] for side in range(sides)]
    weights, rest = rest[3 * sides : 3 * sides + 6], rest[3 * sides + 6 :]
    keep = len(rest) == 1 + sides
    if keep:
        row_out, *panels = rest
    else:
        others, panels, row_out, col_outs = rest[0], rest[1 : 1 + sides], rest[1 + sides], rest[2 + sides :]
    width = weights[0].shape[0]
    own = rows.shape[1] - width
    for at in range(0, rows.shape[0], chunk_rows):
        here = pl.ds(at, chunk_rows)
        block = rows[here, :]
        row_feats = embed(block[:, :width], 1, *weights)
        row_half = 0.5 * jnp.sum(jnp.square(row_feats.astype(F32)), axis=1, keepdims=True)
        row_acc = None
        for side, (feats, half_sq, col_vecs) in enumerate(columns):
            for start in range(0, feats.shape[1], chunk_cols):
                part = pl.ds(start, chunk_cols)
                inner = dot(row_feats, feats[:, part], ((1,), (0,)))
                kernel = jnp.exp(inner - row_half - half_sq[:, part]).astype(BF16)
                term = dot(kernel, col_vecs[:, part], ((1,), (1,)))
                row_acc = term if row_acc is None else row_acc + term
                if keep:
                    panels[side][here, part] = kernel
                else:
                    col_term = dot(block[:, width:], kernel, ((0,), (0,)))
                    col_term += dot(others[here, width:], panels[side][here, part], ((0,), (0,)))
                    if at > 0:
                        col_term += col_outs[side][:, part]
                    col_outs[side][:, part] = col_term
        for start in range(0, chunk_rows, 2 * tall):
            to = pl.ds((at + start) // 2, tall)
            row_out[to, :own] = row_acc[start : start + tall]
            row_out[to, own:] = row_acc[start + tall : start + 2 * tall]


def call(kernel, outs, args, flops):
    return pl.pallas_call(
        kernel,
        out_shape=outs,
        in_specs=[pl.BlockSpec(memory_space=pltpu.VMEM)] * len(args),
        out_specs=[pl.BlockSpec(memory_space=pltpu.VMEM)] * len(outs),
        compiler_params=pltpu.CompilerParams(vmem_limit_bytes=20 * 2**20),
        cost_estimate=pl.CostEstimate(flops=flops, bytes_accessed=2**20, transcendentals=0),
    )(*args)


def hold_kernel(rows, out):
    out[...] = rows[...]


def finish_kernel(scale, own, got, result):
    result[...] = (own[...] + got[...]) * scale[...]


def finish_rows_kernel(scale, own, got, result):
    tall, width = got.shape[0], result.shape[1]
    total = (own[:tall, :] + got[...]) * scale[...]
    result[:tall, :] = total[:, :width]
    result[tall:, :] = total[:, width:]


def body(
    row_points,
    col_points,
    row_vectors,
    col_vectors,
    weight_in,
    bias_in,
    weight_mid,
    bias_mid,
    weight_out,
    ard_scales,
    signal_scale,
):
    count_row, count_col = lax.axis_size("row"), lax.axis_size("col")
    devices = count_row * count_col
    row_masks = [1 << b for b in reversed(range(count_col.bit_length() - 1))] + [devices // 2]
    col_masks = [count_col << b for b in reversed(range(count_row.bit_length() - 2))]

    def swap(block, mask):
        return lax.ppermute(block, AXES, [(i, i ^ mask) for i in range(devices)])

    weights = (
        weight_in,
        bias_in.reshape(1, -1),
        weight_mid,
        bias_mid.reshape(1, -1),
        weight_out,
        ard_scales.reshape(1, -1),
        signal_scale.reshape(1, 1),
    )
    block, nvec = row_vectors.shape
    emb = weight_out.shape[1]
    layers = sum(w.shape[0] * w.shape[1] for w in (weight_in, weight_mid, weight_out))
    chunk_cols = min(512, col_points.shape[0])

    def col_feats(points):
        count = points.shape[1]
        return call(
            functools.partial(col_kernel, chunk_cols),
            [jax.ShapeDtypeStruct((emb, count), BF16), jax.ShapeDtypeStruct((1, count), F32)],
            (points, *weights),
            2 * count * layers,
        )

    *weights, scale = weights
    rows = jnp.concatenate([row_points, row_vectors], axis=1)
    (got,) = call(hold_kernel, [jax.ShapeDtypeStruct(rows.shape, BF16)], (swap(rows, row_masks[0]),), HOLD_FLOPS)
    rows = jnp.concatenate([rows, got], axis=0)
    for mask in row_masks[1:-2]:
        rows = jnp.concatenate([rows, swap(rows, mask)], axis=0)
    points, vectors = [col_points.T], [col_vectors.T]
    for mask in col_masks:
        points.append(swap(jnp.concatenate(points, axis=1), mask))
    feats = [col_feats(points[0])]
    got, feats = lax.optimization_barrier((swap(rows, row_masks[-2]), feats))
    rows = jnp.concatenate([rows, got], axis=0)
    far_rows = swap(rows, row_masks[-1])
    feats += [col_feats(p) for p in points[1:]]
    for mask in col_masks:
        vectors.append(jnp.concatenate([swap(v, mask) for v in vectors], axis=1))
    far_rows, feats = lax.optimization_barrier((far_rows, feats))

    count_rows = rows.shape[0]
    sides = [v.shape[1] for v in vectors]
    panel = functools.partial(panel_kernel, min(4 * block, count_rows), chunk_cols, block // 2, len(sides))
    columns = [a for f, v in zip(feats, vectors, strict=True) for a in (*f, v)]
    flops = 2 * count_rows * (layers + sum(sides) * (emb + 4 * nvec))
    sums = jax.ShapeDtypeStruct((count_rows // 2, 2 * nvec), F32)
    far_panels = [jax.ShapeDtypeStruct((count_rows, count), BF16) for count in sides]
    row_far, *far_panels = call(panel, [sums, *far_panels], (far_rows, *columns, *weights), flops)
    col_sums = [jax.ShapeDtypeStruct((nvec, count), F32) for count in sides]
    args = (rows, *columns, *weights, far_rows, *far_panels)
    row_near, *col_sums = call(panel, [sums, *col_sums], args, flops)

    top = math.ceil(math.log2(CUT_MOST * col_vectors.shape[0] * devices))
    gain = 2.0 ** (math.floor(math.log2(float(jnp.finfo(jnp.float16).max))) - top)

    def swap_sums(block, mask):
        return swap((block * gain).astype(jnp.float16), mask)

    def widen(block):
        return block.astype(F32) * (1.0 / gain)

    got, col_sums = lax.optimization_barrier((swap_sums(row_far, row_masks[-1]), col_sums))
    got = widen(got)
    row_sum = row_near + got
    for number, mask in reversed(list(enumerate(col_masks))[1:]):
        got, start = swap(col_sums[number + 1], mask), 0
        for side in range(number + 1):
            col_sums[side] = col_sums[side] + got[:, start : start + sides[side]]
            start += sides[side]
    got_cols = swap(col_sums[1], col_masks[0])
    own_cols = col_sums[0]
    for mask in reversed(row_masks[1:-1]):
        keep, give = jnp.split(row_sum, 2, axis=0)
        got, own_cols = lax.optimization_barrier((swap_sums(give, mask), own_cols))
        row_sum = keep + widen(got)
    (col_result,) = call(
        finish_kernel, [jax.ShapeDtypeStruct(got_cols.shape, F32)], (scale, own_cols, got_cols), FINISH_FLOPS
    )
    got, col_result = lax.optimization_barrier((swap_sums(row_sum[block // 2 :], row_masks[0]), col_result))
    got = widen(got)
    (row_result,) = call(
        finish_rows_kernel, [jax.ShapeDtypeStruct((block, nvec), F32)], (scale, row_sum, got), FINISH_FLOPS
    )
    return (row_result, col_result.T)


def solution(mesh):
    in_specs = (
        P(("row", "col"), None),
        P(("col", "row"), None),
        P(("row", "col"), None),
        P(("col", "row"), None),
        P(),
        P(),
        P(),
        P(),
        P(),
        P(),
        P(),
    )
    out_specs = (P(("row", "col"), None), P(("col", "row"), None))
    return jax.shard_map(body, mesh=mesh, in_specs=in_specs, out_specs=out_specs, check_vma=False)
```

```python
import functools
import math

import jax
import jax.numpy as jnp
from jax import lax
from jax.experimental import pallas as pl
from jax.experimental.pallas import tpu as pltpu
from jax.sharding import PartitionSpec as P

AXES = ("row", "col")
F32, BF16 = jnp.float32, jnp.bfloat16
HOLD_FLOPS = 2 * 10**10
CUT_MOST = 0.375 * 1.0625
FINISH_FLOPS = 10**6


def dot(a, b, over):
    return lax.dot_general(a, b, (over, ((), ())), preferred_element_type=F32)


def embed(points, over, w_in, b_in, w_mid, b_mid, w_out, ard):
    one = jnp.tanh(dot(points, w_in[...], ((over,), (0,))) + b_in[...]).astype(BF16)
    two = jnp.tanh(dot(one, w_mid[...], ((1,), (0,))) + b_mid[...]).astype(BF16)
    return (dot(two, w_out[...], ((1,), (0,))) * jnp.sqrt(ard[...])).astype(BF16)


def col_kernel(chunk, points, *rest):
    weights, (feats, half_sq) = rest[:6], rest[-2:]
    for start in range(0, points.shape[1], chunk):
        part = pl.ds(start, chunk)
        turned = embed(points[:, part], 0, *weights).T
        feats[:, part] = turned
        half_sq[:, part] = 0.5 * jnp.sum(jnp.square(turned.astype(F32)), axis=0, keepdims=True)


def panel_kernel(chunk_rows, chunk_cols, tall, sides, rows, *rest):
    columns = [rest[3 * side : 3 * side + 3] for side in range(sides)]
    weights, rest = rest[3 * sides : 3 * sides + 6], rest[3 * sides + 6 :]
    keep = len(rest) == 1 + sides
    if keep:
        row_out, *panels = rest
    else:
        others, panels, row_out, col_outs = rest[0], rest[1 : 1 + sides], rest[1 + sides], rest[2 + sides :]
    width = weights[0].shape[0]
    own = rows.shape[1] - width
    for at in range(0, rows.shape[0], chunk_rows):
        here = pl.ds(at, chunk_rows)
        block = rows[here, :]
        row_feats = embed(block[:, :width], 1, *weights)
        row_half = 0.5 * jnp.sum(jnp.square(row_feats.astype(F32)), axis=1, keepdims=True)
        row_acc = None
        for side, (feats, half_sq, col_vecs) in enumerate(columns):
            for start in range(0, feats.shape[1], chunk_cols):
                part = pl.ds(start, chunk_cols)
                inner = dot(row_feats, feats[:, part], ((1,), (0,)))
                kernel = jnp.exp(inner - row_half - half_sq[:, part]).astype(BF16)
                term = dot(kernel, col_vecs[:, part], ((1,), (1,)))
                row_acc = term if row_acc is None else row_acc + term
                if keep:
                    panels[side][here, part] = kernel
                else:
                    col_term = dot(block[:, width:], kernel, ((0,), (0,)))
                    col_term += dot(others[here, width:], panels[side][here, part], ((0,), (0,)))
                    if at > 0:
                        col_term += col_outs[side][:, part]
                    col_outs[side][:, part] = col_term
        for start in range(0, chunk_rows, 2 * tall):
            to = pl.ds((at + start) // 2, tall)
            row_out[to, :own] = row_acc[start : start + tall]
            row_out[to, own:] = row_acc[start + tall : start + 2 * tall]


def call(kernel, outs, args, flops):
    return pl.pallas_call(
        kernel,
        out_shape=outs,
        in_specs=[pl.BlockSpec(memory_space=pltpu.SMEM if a.shape == (1,) else pltpu.VMEM) for a in args],
        out_specs=[pl.BlockSpec(memory_space=pltpu.VMEM)] * len(outs),
        compiler_params=pltpu.CompilerParams(vmem_limit_bytes=20 * 2**20),
        cost_estimate=pl.CostEstimate(flops=flops, bytes_accessed=2**20, transcendentals=0),
    )(*args)


def hold_kernel(rows, out):
    out[...] = rows[...]


def finish_kernel(scale, own, got, result):
    result[...] = (own[...] + got[...]) * scale[0]


def finish_rows_kernel(scale, own, got, result):
    tall, width = got.shape[0], result.shape[1]
    total = (own[:tall, :] + got[...]) * scale[0]
    result[:tall, :] = total[:, :width]
    result[tall:, :] = total[:, width:]


def body(
    row_points,
    col_points,
    row_vectors,
    col_vectors,
    weight_in,
    bias_in,
    weight_mid,
    bias_mid,
    weight_out,
    ard_scales,
    signal_scale,
):
    count_row, count_col = lax.axis_size("row"), lax.axis_size("col")
    devices = count_row * count_col
    row_masks = [(1 << b) | count_col for b in reversed(range(count_col.bit_length() - 1))] + [(devices // 2) | count_col]
    col_masks = [(count_col << b) | count_col for b in reversed(range(count_row.bit_length() - 2))]

    def swap(block, mask):
        return lax.ppermute(block, AXES, [(i, i ^ mask) for i in range(devices)])

    weights = (
        weight_in,
        bias_in.reshape(1, -1),
        weight_mid,
        bias_mid.reshape(1, -1),
        weight_out,
        ard_scales.reshape(1, -1),
    )
    block, nvec = row_vectors.shape
    emb = weight_out.shape[1]
    layers = sum(w.shape[0] * w.shape[1] for w in (weight_in, weight_mid, weight_out))
    chunk_cols = min(512, col_points.shape[0])

    def col_feats(points):
        count = points.shape[1]
        return call(
            functools.partial(col_kernel, chunk_cols),
            [jax.ShapeDtypeStruct((emb, count), BF16), jax.ShapeDtypeStruct((1, count), F32)],
            (points, *weights),
            2 * count * layers,
        )

    rows = lax.optimization_barrier(jnp.concatenate([row_points, row_vectors], axis=1))
    (got,) = call(hold_kernel, [jax.ShapeDtypeStruct(rows.shape, BF16)], (swap(rows, row_masks[0]),), HOLD_FLOPS)
    rows = jnp.concatenate([rows, got], axis=0)
    for mask in row_masks[1:-2]:
        rows = jnp.concatenate([rows, swap(rows, mask)], axis=0)
    points, vectors = [col_points.T], [col_vectors.T]
    for mask in col_masks:
        points.append(swap(jnp.concatenate(points, axis=1), mask))
    feats = [col_feats(points[0])]
    got, feats = lax.optimization_barrier((swap(rows, row_masks[-2]), feats))
    rows = jnp.concatenate([rows, got], axis=0)
    far_rows = swap(rows, row_masks[-1])
    feats += [col_feats(p) for p in points[1:]]
    for mask in col_masks:
        vectors.append(jnp.concatenate([swap(v, mask) for v in vectors], axis=1))
    far_rows, feats = lax.optimization_barrier((far_rows, feats))

    count_rows = rows.shape[0]
    sides = [v.shape[1] for v in vectors]
    panel = functools.partial(panel_kernel, min(4 * block, count_rows), chunk_cols, block // 2, len(sides))
    columns = [a for f, v in zip(feats, vectors, strict=True) for a in (*f, v)]
    flops = 2 * count_rows * (layers + sum(sides) * (emb + 4 * nvec))
    sums = jax.ShapeDtypeStruct((count_rows // 2, 2 * nvec), F32)
    far_panels = [jax.ShapeDtypeStruct((count_rows, count), BF16) for count in sides]
    row_far, *far_panels = call(panel, [sums, *far_panels], (far_rows, *columns, *weights), flops)
    col_sums = [jax.ShapeDtypeStruct((nvec, count), F32) for count in sides]
    args = (rows, *columns, *weights, far_rows, *far_panels)
    row_near, *col_sums = call(panel, [sums, *col_sums], args, flops)

    top = math.ceil(math.log2(CUT_MOST * col_vectors.shape[0] * devices))
    gain = 2.0 ** (math.floor(math.log2(float(jnp.finfo(jnp.float16).max))) - top)

    def swap_sums(block, mask):
        return swap((block * gain).astype(jnp.float16), mask)

    def widen(block):
        return block.astype(F32) * (1.0 / gain)

    got, col_sums = lax.optimization_barrier((swap_sums(row_far, row_masks[-1]), col_sums))
    got = widen(got)
    row_sum = row_near + got
    for number, mask in reversed(list(enumerate(col_masks))[1:]):
        got, start = swap(col_sums[number + 1], mask), 0
        for side in range(number + 1):
            col_sums[side] = col_sums[side] + got[:, start : start + sides[side]]
            start += sides[side]
    got_cols = swap(col_sums[1], col_masks[0])
    own_cols = col_sums[0]
    for mask in reversed(row_masks[1:-1]):
        keep, give = jnp.split(row_sum, 2, axis=0)
        got, own_cols = lax.optimization_barrier((swap_sums(give, mask), own_cols))
        row_sum = keep + widen(got)
    (col_result,) = call(
        finish_kernel, [jax.ShapeDtypeStruct(got_cols.shape, F32)], (signal_scale, own_cols, got_cols), FINISH_FLOPS
    )
    got, col_result = lax.optimization_barrier((swap_sums(row_sum[block // 2 :], row_masks[0]), col_result))
    got = widen(got)
    (row_result,) = call(
        finish_rows_kernel, [jax.ShapeDtypeStruct((block, nvec), F32)], (signal_scale, row_sum, got), FINISH_FLOPS
    )
    return (row_result, col_result.T)


def solution(mesh):
    in_specs = (
        P(("row", "col"), None),
        P(("col", "row"), None),
        P(("row", "col"), None),
        P(("col", "row"), None),
        P(),
        P(),
        P(),
        P(),
        P(),
        P(),
        P(),
    )
    out_specs = (P(("row", "col"), None), P(("col", "row"), None))
    return jax.shard_map(body, mesh=mesh, in_specs=in_specs, out_specs=out_specs, check_vma=False)
```

```python
import functools
import math

import jax
import jax.numpy as jnp
from jax import lax
from jax.experimental import pallas as pl
from jax.experimental.pallas import tpu as pltpu
from jax.sharding import PartitionSpec as P

AXES = ("row", "col")
F32, BF16 = jnp.float32, jnp.bfloat16
HOLD_FLOPS = 2 * 10**10
CUT_MOST = 0.375 * 1.0625
FINISH_FLOPS = 10**6


def dot(a, b, over):
    return lax.dot_general(a, b, (over, ((), ())), preferred_element_type=F32)


def embed(points, over, w_in, b_in, w_mid, b_mid, w_out, ard):
    one = jnp.tanh(dot(points, w_in[...], ((over,), (0,))) + b_in[...]).astype(BF16)
    two = jnp.tanh(dot(one, w_mid[...], ((1,), (0,))) + b_mid[...]).astype(BF16)
    return (dot(two, w_out[...], ((1,), (0,))) * jnp.sqrt(ard[...])).astype(BF16)


def col_kernel(chunk, points, *rest):
    weights, (feats, half_sq) = rest[:6], rest[-2:]
    for start in range(0, points.shape[1], chunk):
        part = pl.ds(start, chunk)
        turned = embed(points[:, part], 0, *weights).T
        feats[:, part] = turned
        half_sq[:, part] = 0.5 * jnp.sum(jnp.square(turned.astype(F32)), axis=0, keepdims=True)


def panel_kernel(chunk_rows, chunk_cols, tall, sides, rows, *rest):
    columns = [rest[3 * side : 3 * side + 3] for side in range(sides)]
    weights, rest = rest[3 * sides : 3 * sides + 6], rest[3 * sides + 6 :]
    keep = len(rest) == 1 + sides
    if keep:
        row_out, *panels = rest
    else:
        others, panels, row_out, col_outs = rest[0], rest[1 : 1 + sides], rest[1 + sides], rest[2 + sides :]
    width = weights[0].shape[0]
    own = rows.shape[1] - width
    for at in range(0, rows.shape[0], chunk_rows):
        here = pl.ds(at, chunk_rows)
        block = rows[here, :]
        row_feats = embed(block[:, :width], 1, *weights)
        row_half = 0.5 * jnp.sum(jnp.square(row_feats.astype(F32)), axis=1, keepdims=True)
        row_acc = None
        for side, (feats, half_sq, col_vecs) in enumerate(columns):
            for start in range(0, feats.shape[1], chunk_cols):
                part = pl.ds(start, chunk_cols)
                inner = dot(row_feats, feats[:, part], ((1,), (0,)))
                kernel = jnp.exp(inner - row_half - half_sq[:, part]).astype(BF16)
                term = dot(kernel, col_vecs[:, part], ((1,), (1,)))
                row_acc = term if row_acc is None else row_acc + term
                if keep:
                    panels[side][here, part] = kernel
                else:
                    col_term = dot(block[:, width:], kernel, ((0,), (0,)))
                    col_term += dot(others[here, width:], panels[side][here, part], ((0,), (0,)))
                    if at > 0:
                        col_term += col_outs[side][:, part]
                    col_outs[side][:, part] = col_term
        for start in range(0, chunk_rows, 2 * tall):
            to = pl.ds((at + start) // 2, tall)
            row_out[to, :own] = row_acc[start : start + tall]
            row_out[to, own:] = row_acc[start + tall : start + 2 * tall]


def call(kernel, outs, args, flops):
    return pl.pallas_call(
        kernel,
        out_shape=outs,
        in_specs=[pl.BlockSpec(memory_space=pltpu.SMEM if a.shape == (1,) else pltpu.VMEM) for a in args],
        out_specs=[pl.BlockSpec(memory_space=pltpu.VMEM)] * len(outs),
        compiler_params=pltpu.CompilerParams(vmem_limit_bytes=20 * 2**20),
        cost_estimate=pl.CostEstimate(flops=flops, bytes_accessed=2**20, transcendentals=0),
    )(*args)


def hold_kernel(rows, out):
    out[...] = rows[...]


def finish_kernel(scale, own_cols, got_cols, own_rows, got_rows, col_result, row_result):
    col_result[...] = (own_cols[...] + got_cols[...]) * scale[0]
    tall, width = got_rows.shape[0], row_result.shape[1]
    total = (own_rows[:tall, :] + got_rows[...]) * scale[0]
    row_result[:tall, :] = total[:, :width]
    row_result[tall:, :] = total[:, width:]


def body(
    row_points,
    col_points,
    row_vectors,
    col_vectors,
    weight_in,
    bias_in,
    weight_mid,
    bias_mid,
    weight_out,
    ard_scales,
    signal_scale,
):
    count_row, count_col = lax.axis_size("row"), lax.axis_size("col")
    devices = count_row * count_col
    row_masks = [(1 << b) | count_col for b in reversed(range(count_col.bit_length() - 1))] + [(devices // 2) | count_col]
    col_masks = [(count_col << b) | count_col for b in reversed(range(count_row.bit_length() - 2))]

    def swap(block, mask):
        return lax.ppermute(block, AXES, [(i, i ^ mask) for i in range(devices)])

    weights = (
        weight_in,
        bias_in.reshape(1, -1),
        weight_mid,
        bias_mid.reshape(1, -1),
        weight_out,
        ard_scales.reshape(1, -1),
    )
    block, nvec = row_vectors.shape
    emb = weight_out.shape[1]
    layers = sum(w.shape[0] * w.shape[1] for w in (weight_in, weight_mid, weight_out))
    chunk_cols = min(512, col_points.shape[0])

    def col_feats(points):
        count = points.shape[1]
        return call(
            functools.partial(col_kernel, chunk_cols),
            [jax.ShapeDtypeStruct((emb, count), BF16), jax.ShapeDtypeStruct((1, count), F32)],
            (points, *weights),
            2 * count * layers,
        )

    rows = lax.optimization_barrier(jnp.concatenate([row_points, row_vectors], axis=1))
    (got,) = call(hold_kernel, [jax.ShapeDtypeStruct(rows.shape, BF16)], (swap(rows, row_masks[0]),), HOLD_FLOPS)
    rows = jnp.concatenate([rows, got], axis=0)
    for mask in row_masks[1:-2]:
        rows = jnp.concatenate([rows, swap(rows, mask)], axis=0)
    points, vectors = [col_points.T], [col_vectors.T]
    for mask in col_masks:
        points.append(swap(jnp.concatenate(points, axis=1), mask))
    feats = [col_feats(points[0])]
    got, feats = lax.optimization_barrier((swap(rows, row_masks[-2]), feats))
    rows = jnp.concatenate([rows, got], axis=0)
    far_rows = swap(rows, row_masks[-1])
    feats += [col_feats(p) for p in points[1:]]
    for mask in col_masks:
        vectors.append(jnp.concatenate([swap(v, mask) for v in vectors], axis=1))
    far_rows, feats = lax.optimization_barrier((far_rows, feats))

    count_rows = rows.shape[0]
    sides = [v.shape[1] for v in vectors]
    panel = functools.partial(panel_kernel, min(4 * block, count_rows), chunk_cols, block // 2, len(sides))
    columns = [a for f, v in zip(feats, vectors, strict=True) for a in (*f, v)]
    flops = 2 * count_rows * (layers + sum(sides) * (emb + 4 * nvec))
    sums = jax.ShapeDtypeStruct((count_rows // 2, 2 * nvec), F32)
    far_panels = [jax.ShapeDtypeStruct((count_rows, count), BF16) for count in sides]
    row_far, *far_panels = call(panel, [sums, *far_panels], (far_rows, *columns, *weights), flops)
    col_sums = [jax.ShapeDtypeStruct((nvec, count), F32) for count in sides]
    args = (rows, *columns, *weights, far_rows, *far_panels)
    row_near, *col_sums = call(panel, [sums, *col_sums], args, flops)

    top = math.ceil(math.log2(CUT_MOST * col_vectors.shape[0] * devices))
    gain = 2.0 ** (math.floor(math.log2(float(jnp.finfo(jnp.float16).max))) - top)

    def swap_sums(block, mask):
        return swap((block * gain).astype(jnp.float16), mask)

    def widen(block):
        return block.astype(F32) * (1.0 / gain)

    got, col_sums = lax.optimization_barrier((swap_sums(row_far, row_masks[-1]), col_sums))
    got = widen(got)
    row_sum = row_near + got
    for number, mask in reversed(list(enumerate(col_masks))[1:]):
        got, start = swap(col_sums[number + 1], mask), 0
        for side in range(number + 1):
            col_sums[side] = col_sums[side] + got[:, start : start + sides[side]]
            start += sides[side]
    got_cols = swap(col_sums[1], col_masks[0])
    own_cols = col_sums[0]
    for mask in reversed(row_masks[1:-1]):
        keep, give = jnp.split(row_sum, 2, axis=0)
        got, own_cols = lax.optimization_barrier((swap_sums(give, mask), own_cols))
        row_sum = keep + widen(got)
    got = swap_sums(row_sum[block // 2 :], row_masks[0])
    got, got_cols = lax.optimization_barrier((got, got_cols))
    col_result, row_result = call(
        finish_kernel,
        [jax.ShapeDtypeStruct(got_cols.shape, F32), jax.ShapeDtypeStruct((block, nvec), F32)],
        (signal_scale, own_cols, got_cols, row_sum, widen(got)),
        FINISH_FLOPS,
    )
    return (row_result, col_result.T)


def solution(mesh):
    in_specs = (
        P(("row", "col"), None),
        P(("col", "row"), None),
        P(("row", "col"), None),
        P(("col", "row"), None),
        P(),
        P(),
        P(),
        P(),
        P(),
        P(),
        P(),
    )
    out_specs = (P(("row", "col"), None), P(("col", "row"), None))
    return jax.shard_map(body, mesh=mesh, in_specs=in_specs, out_specs=out_specs, check_vma=False)
```

```python
import functools
import math

import jax
import jax.numpy as jnp
from jax import lax
from jax.experimental import pallas as pl
from jax.experimental.pallas import tpu as pltpu
from jax.sharding import PartitionSpec as P

AXES = ("row", "col")
F32, BF16 = jnp.float32, jnp.bfloat16
HOLD_FLOPS = 2 * 10**10
CUT_MOST = 0.375 * 1.0625
FINISH_FLOPS = 10**6


def dot(a, b, over):
    return lax.dot_general(a, b, (over, ((), ())), preferred_element_type=F32)


def embed(points, over, w_in, b_in, w_mid, b_mid, w_out, ard):
    one = jnp.tanh(dot(points, w_in[...], ((over,), (0,))) + b_in[...]).astype(BF16)
    two = jnp.tanh(dot(one, w_mid[...], ((1,), (0,))) + b_mid[...]).astype(BF16)
    return (dot(two, w_out[...], ((1,), (0,))) * jnp.sqrt(ard[...])).astype(BF16)


def col_kernel(chunk, points, *rest):
    weights, (feats, half_sq) = rest[:6], rest[-2:]
    for start in range(0, points.shape[1], chunk):
        part = pl.ds(start, chunk)
        turned = embed(points[:, part], 0, *weights).T
        feats[:, part] = turned
        half_sq[:, part] = 0.5 * jnp.sum(jnp.square(turned.astype(F32)), axis=0, keepdims=True)


def panel_kernel(chunk_rows, chunk_cols, tall, sides, rows, *rest):
    columns = [rest[3 * side : 3 * side + 3] for side in range(sides)]
    weights, rest = rest[3 * sides : 3 * sides + 6], rest[3 * sides + 6 :]
    keep = len(rest) == 1 + sides
    if keep:
        row_out, *panels = rest
    else:
        others, panels, row_out, col_outs = rest[0], rest[1 : 1 + sides], rest[1 + sides], rest[2 + sides :]
    width = weights[0].shape[0]
    own = rows.shape[1] - width
    for at in range(0, rows.shape[0], chunk_rows):
        here = pl.ds(at, chunk_rows)
        block = rows[here, :]
        row_feats = embed(block[:, :width], 1, *weights)
        row_half = 0.5 * jnp.sum(jnp.square(row_feats.astype(F32)), axis=1, keepdims=True)
        row_acc = None
        for side, (feats, half_sq, col_vecs) in enumerate(columns):
            wide = min(2 * chunk_cols, feats.shape[1])
            for start in range(0, feats.shape[1], wide):
                part = pl.ds(start, wide)
                inner = dot(row_feats, feats[:, part], ((1,), (0,)))
                kernel = jnp.exp(inner - row_half - half_sq[:, part]).astype(BF16)
                term = dot(kernel, col_vecs[:, part], ((1,), (1,)))
                row_acc = term if row_acc is None else row_acc + term
                if keep:
                    panels[side][here, part] = kernel
                else:
                    col_term = dot(block[:, width:], kernel, ((0,), (0,)))
                    col_term += dot(others[here, width:], panels[side][here, part], ((0,), (0,)))
                    if at > 0:
                        col_term += col_outs[side][:, part]
                    col_outs[side][:, part] = col_term
        for start in range(0, chunk_rows, 2 * tall):
            to = pl.ds((at + start) // 2, tall)
            row_out[to, :own] = row_acc[start : start + tall]
            row_out[to, own:] = row_acc[start + tall : start + 2 * tall]


def call(kernel, outs, args, flops):
    return pl.pallas_call(
        kernel,
        out_shape=outs,
        in_specs=[pl.BlockSpec(memory_space=pltpu.SMEM if a.shape == (1,) else pltpu.VMEM) for a in args],
        out_specs=[pl.BlockSpec(memory_space=pltpu.VMEM)] * len(outs),
        compiler_params=pltpu.CompilerParams(vmem_limit_bytes=20 * 2**20),
        cost_estimate=pl.CostEstimate(flops=flops, bytes_accessed=2**20, transcendentals=0),
    )(*args)


def hold_kernel(rows, out):
    out[...] = rows[...]


def finish_kernel(scale, own_cols, got_cols, own_rows, got_rows, col_result, row_result):
    col_result[...] = (own_cols[...] + got_cols[...]) * scale[0]
    tall, width = got_rows.shape[0], row_result.shape[1]
    total = (own_rows[:tall, :] + got_rows[...]) * scale[0]
    row_result[:tall, :] = total[:, :width]
    row_result[tall:, :] = total[:, width:]


def body(
    row_points,
    col_points,
    row_vectors,
    col_vectors,
    weight_in,
    bias_in,
    weight_mid,
    bias_mid,
    weight_out,
    ard_scales,
    signal_scale,
):
    count_row, count_col = lax.axis_size("row"), lax.axis_size("col")
    devices = count_row * count_col
    row_masks = [(1 << b) | count_col for b in reversed(range(count_col.bit_length() - 1))] + [(devices // 2) | count_col]
    col_masks = [(count_col << b) | count_col for b in reversed(range(count_row.bit_length() - 2))]

    def swap(block, mask):
        return lax.ppermute(block, AXES, [(i, i ^ mask) for i in range(devices)])

    weights = (
        weight_in,
        bias_in.reshape(1, -1),
        weight_mid,
        bias_mid.reshape(1, -1),
        weight_out,
        ard_scales.reshape(1, -1),
    )
    block, nvec = row_vectors.shape
    emb = weight_out.shape[1]
    layers = sum(w.shape[0] * w.shape[1] for w in (weight_in, weight_mid, weight_out))
    chunk_cols = min(512, col_points.shape[0])

    def col_feats(points):
        count = points.shape[1]
        return call(
            functools.partial(col_kernel, chunk_cols),
            [jax.ShapeDtypeStruct((emb, count), BF16), jax.ShapeDtypeStruct((1, count), F32)],
            (points, *weights),
            2 * count * layers,
        )

    rows = lax.optimization_barrier(jnp.concatenate([row_points, row_vectors], axis=1))
    (got,) = call(hold_kernel, [jax.ShapeDtypeStruct(rows.shape, BF16)], (swap(rows, row_masks[0]),), HOLD_FLOPS)
    rows = jnp.concatenate([rows, got], axis=0)
    for mask in row_masks[1:-2]:
        rows = jnp.concatenate([rows, swap(rows, mask)], axis=0)
    points, vectors = [col_points.T], [col_vectors.T]
    for mask in col_masks:
        points.append(swap(jnp.concatenate(points, axis=1), mask))
    feats = [col_feats(points[0])]
    got, feats = lax.optimization_barrier((swap(rows, row_masks[-2]), feats))
    rows = jnp.concatenate([rows, got], axis=0)
    far_rows = swap(rows, row_masks[-1])
    feats += [col_feats(p) for p in points[1:]]
    for mask in col_masks:
        vectors.append(jnp.concatenate([swap(v, mask) for v in vectors], axis=1))
    far_rows, feats = lax.optimization_barrier((far_rows, feats))

    count_rows = rows.shape[0]
    sides = [v.shape[1] for v in vectors]
    panel = functools.partial(panel_kernel, min(4 * block, count_rows), chunk_cols, block // 2, len(sides))
    columns = [a for f, v in zip(feats, vectors, strict=True) for a in (*f, v)]
    flops = 2 * count_rows * (layers + sum(sides) * (emb + 4 * nvec))
    sums = jax.ShapeDtypeStruct((count_rows // 2, 2 * nvec), F32)
    far_panels = [jax.ShapeDtypeStruct((count_rows, count), BF16) for count in sides]
    row_far, *far_panels = call(panel, [sums, *far_panels], (far_rows, *columns, *weights), flops)
    col_sums = [jax.ShapeDtypeStruct((nvec, count), F32) for count in sides]
    args = (rows, *columns, *weights, far_rows, *far_panels)
    row_near, *col_sums = call(panel, [sums, *col_sums], args, flops)

    top = math.ceil(math.log2(CUT_MOST * col_vectors.shape[0] * devices))
    gain = 2.0 ** (math.floor(math.log2(float(jnp.finfo(jnp.float16).max))) - top)

    def swap_sums(block, mask):
        return swap((block * gain).astype(jnp.float16), mask)

    def widen(block):
        return block.astype(F32) * (1.0 / gain)

    got, col_sums = lax.optimization_barrier((swap_sums(row_far, row_masks[-1]), col_sums))
    got = widen(got)
    row_sum = row_near + got
    for number, mask in reversed(list(enumerate(col_masks))[1:]):
        got, start = swap(col_sums[number + 1], mask), 0
        for side in range(number + 1):
            col_sums[side] = col_sums[side] + got[:, start : start + sides[side]]
            start += sides[side]
    got_cols = swap(col_sums[1], col_masks[0])
    own_cols = col_sums[0]
    for mask in reversed(row_masks[1:-1]):
        keep, give = jnp.split(row_sum, 2, axis=0)
        got, own_cols = lax.optimization_barrier((swap_sums(give, mask), own_cols))
        row_sum = keep + widen(got)
    got = swap_sums(row_sum[block // 2 :], row_masks[0])
    got, got_cols = lax.optimization_barrier((got, got_cols))
    col_result, row_result = call(
        finish_kernel,
        [jax.ShapeDtypeStruct(got_cols.shape, F32), jax.ShapeDtypeStruct((block, nvec), F32)],
        (signal_scale, own_cols, got_cols, row_sum, widen(got)),
        FINISH_FLOPS,
    )
    return (row_result, col_result.T)


def solution(mesh):
    in_specs = (
        P(("row", "col"), None),
        P(("col", "row"), None),
        P(("row", "col"), None),
        P(("col", "row"), None),
        P(),
        P(),
        P(),
        P(),
        P(),
        P(),
        P(),
    )
    out_specs = (P(("row", "col"), None), P(("col", "row"), None))
    return jax.shard_map(body, mesh=mesh, in_specs=in_specs, out_specs=out_specs, check_vma=False)
```
